512 devices in a mesh: section: 8 (over x, core), expert: 64 (over z, y).
Axes of the slice: x: 4, y: 8, z: 8, core: 2. Of those that a mesh axis runs over, the one named last changes fastest.
Arguments:
- tokens: bfloat16 [8, 128, 3072], P('section'), may hold values from -6 to 6
- gains: bfloat16 [3072], replicated, may hold values from 0.25 to 1.75
- w_router: bfloat16 [3072, 8], replicated, may hold values from -0.109375 to 0.109375
- w_gate: bfloat16 [8, 3072, 8192], P('section', None, 'expert'), may hold values from -0.109375 to 0.109375
- w_up: bfloat16 [8, 3072, 8192], P('section', None, 'expert'), may hold values from -0.109375 to 0.109375
- w_down: bfloat16 [8, 3072, 8192], P('section', 'expert'), may hold values from -0.125 to 0.125
- routing: int32 [8, 128, 2], replicated, may hold values from 0 to 7, all different within a row; in each aligned block of 128 rows (0 to 127, 128 to 255, ..., all dimensions but the last counted through in order) at most 64 rows name the same one
Outputs:
- result: bfloat16 [8, 128, 3072], P('section', None, 'expert')
The draws below stay inside these ranges and needn't reach their ends.
Inputs may be any that keep to these rules, and one draw needn't show every extreme that they name: `routing`: each token names two different experts. In each microbatch no expert is named by more than 64 tokens, a bound that some block reaches.
All inputs are finite; a program needn't handle non-finite values.
Results may differ from the reference program's by a relative error of at most 0.0056.
Values may be sent and summed in bfloat16 or wider, within the bound.
No kernel may reach another device: no remote copies, remote signals or barrier semaphores. Data moves between devices by JAX's collectives and lax.ppermute only.
A program may use at most 64 MiB of HBM per device.

```python
import math
import jax
import jax.numpy as jnp
import numpy as np
from jax import lax

D = 3072
EXPERTS = 8
TOP = 2
FE = 8192
ROWS = 128
CAP = 64
MICRO = 8


def level_of(rng, extent, split, least, top_value):
    def one(position, shards_of):
        steps = jax.random.uniform(jax.random.fold_in(jax.random.fold_in(rng, 6), position), (shards_of,), jnp.float32, least / len(split), top_value / len(split))
        return jnp.repeat(jnp.exp(steps), extent[position] // shards_of).reshape((-1,) + (1,) * (len(extent) - position - 1))

    factor_of = one(*split[0])
    for cut in split[1:]:
        factor_of = factor_of * one(*cut)
    return factor_of


def deal_out(own_key, own, number, rows, count, top, most, skew):
    sequence = jax.random.permutation(own_key, count)
    crowded, usual = load_shares(count, rows * top, most, skew, True), load_shares(count, rows * top, most, skew, False)
    places = jnp.arange(count)

    def named(lengths, turn):
        used = int((lengths > 0).sum())
        fixed = max(1, used // 4)
        passed = fixed + (places - fixed + turn * (used - fixed)) % max(1, count - fixed)
        return jnp.zeros((count,), jnp.int32).at[sequence[jnp.where(places < fixed, places, passed)]].set(jnp.asarray(lengths, jnp.int32))

    lengths = jnp.where(number % 4 == 0, named(crowded, number // 4), named(usual, number - number // 4 - 1))
    mixed = jax.random.permutation(jax.random.fold_in(own, 3), count)
    source_of, receiver = mixed[0:count // 2 * 2:2], mixed[1:count // 2 * 2:2]
    slack = jnp.minimum(lengths[source_of] - 1, most - lengths[receiver]) // 2
    slack = jnp.where((source_of == sequence[0]) | (receiver == sequence[0]) | (lengths[receiver] == 0), 0, jnp.maximum(slack, 0))
    passed = jax.random.randint(jax.random.fold_in(own, 4), (count // 2,), 0, 1 << 20) % (slack + 1)
    lengths = lengths.at[source_of].add(-passed).at[receiver].add(passed)
    members = jnp.searchsorted(jnp.cumsum(lengths), jnp.arange(rows * top), side="right").astype(jnp.int32)
    listing = members.reshape(top, rows).T
    listing = listing[jax.random.permutation(jax.random.fold_in(own, 1), rows)]
    turn = jax.random.randint(jax.random.fold_in(own, 2), (rows, 1), 0, top)
    return jnp.take_along_axis(listing, (jnp.arange(top)[None, :] + turn) % top, axis=1)


def load_shares(count, total, most, skew, full):
    loads = [(1 << 20) // math.isqrt(rank ** skew) + 1 for rank in range(1, count + 1)]
    largest = most if full else min(most, max(-(-total // count), total * loads[0] // sum(loads)))
    least = 1 if total - largest >= count - 1 else 0
    counts, surplus = [largest] + [least] * (count - 1), total - largest - least * (count - 1)
    while surplus > 0:
        candidates = [i for i in range(1, count) if counts[i] < largest] or [i for i in range(1, count) if counts[i] < most]
        pool, left = sum([loads[i] for i in candidates]), surplus
        for i in candidates:
            more = min(most - counts[i], max(1, left * loads[i] // pool), surplus)
            counts[i] = counts[i] + more
            surplus = surplus - more
    return np.array(counts)


def normal_values(rng, dims, width, most, shards=(), kind=jnp.bfloat16):
    result = width * jax.random.normal(rng, dims, jnp.float32)
    if shards:
        result = result * level_of(rng, dims, shards, -0.22, 0.18)
    return jnp.clip(result, -most, most).astype(kind)


def setup_inputs(seed: int = 0) -> dict:
    streams_of = jax.random.split(jax.random.key(seed), 8)
    tokens = normal_values(streams_of[0], (MICRO, ROWS, D), 1.0, 6.0, ((0, 8),))
    gains = jnp.clip(1.0 + 0.15 * jax.random.normal(streams_of[1], (D,), jnp.float32), 0.25, 1.75).astype(jnp.bfloat16)
    w_router = normal_values(streams_of[2], (D, EXPERTS), D ** -0.5, 0.109375)
    w_gate = normal_values(streams_of[3], (EXPERTS, D, FE), D ** -0.5, 0.109375, ((0, 8), (2, 64)))
    w_up = normal_values(streams_of[4], (EXPERTS, D, FE), D ** -0.5, 0.109375, ((0, 8), (2, 64)))
    w_down = normal_values(streams_of[5], (EXPERTS, D, FE), (FE // 4) ** -0.5, 0.125, ((0, 8), (1, 64)))
    routing_keys = jax.random.split(jax.random.fold_in(streams_of[6], 1), MICRO * ROWS // ROWS)
    routing_turns = jax.random.permutation(jax.random.fold_in(streams_of[6], 3), MICRO * ROWS // ROWS)
    routing = jax.vmap(lambda own, number: deal_out(jax.random.fold_in(streams_of[6], 2), own, number, ROWS, EXPERTS, TOP, CAP, 2))(routing_keys, routing_turns).reshape((MICRO, ROWS, TOP))
    return dict(tokens=tokens, gains=gains, w_router=w_router, w_gate=w_gate, w_up=w_up, w_down=w_down, routing=routing)


def norm_rows(values, gain_row):
    widened = values.astype(jnp.float32)
    mean_sq = lax.optimization_barrier(jnp.mean(widened * widened, axis=-1, keepdims=True))
    return (widened * lax.rsqrt(mean_sq + 1e-05) * gain_row.astype(jnp.float32)).astype(jnp.bfloat16)

def expert_shares(normed, router, expert_ids):
    logits = jnp.dot(normed, router, preferred_element_type=jnp.float32)
    picked = jnp.take_along_axis(logits, expert_ids, axis=1)
    margin = picked[:, 0] - picked[:, 1]
    return jnp.stack([jax.nn.sigmoid(margin), jax.nn.sigmoid(-margin)], axis=1)

def reference(tokens, gains, w_router, w_gate, w_up, w_down, routing):
    finished = []
    slot_ids = jnp.arange(CAP, dtype=jnp.int32)
    for micro_index in range(MICRO):
        current = tokens[micro_index]
        expert_ids = routing[micro_index]
        normed = norm_rows(current, gains)
        shares = expert_shares(normed, w_router, expert_ids)
        total_sum = jnp.zeros((ROWS, D), jnp.float32)
        for expert_id in range(EXPERTS):
            matched = expert_ids == expert_id
            chosen = jnp.any(matched, axis=1)
            ranking = (jnp.cumsum(chosen.astype(jnp.int32)) - 1).astype(jnp.int32)
            placing = jnp.logical_and(ranking[None, :] == slot_ids[:, None], chosen[None, :])
            packed = jnp.dot(placing.astype(jnp.bfloat16), normed, preferred_element_type=jnp.float32).astype(jnp.bfloat16)
            gate_pre = jnp.dot(packed, w_gate[expert_id], preferred_element_type=jnp.float32)
            up_proj = jnp.dot(packed, w_up[expert_id], preferred_element_type=jnp.float32)
            hidden = (jax.nn.silu(gate_pre) * up_proj).astype(jnp.bfloat16)
            output = lax.dot_general(hidden, w_down[expert_id], (((1,), (1,)), ((), ())), preferred_element_type=jnp.float32)
            weights = lax.optimization_barrier(jnp.sum(jnp.where(matched, shares, 0.0), axis=1))
            spread = jnp.where(placing, weights[None, :], 0.0)
            total_sum = total_sum + jnp.dot(spread.T, output, precision=lax.Precision.HIGHEST)
        finished.append((current.astype(jnp.float32) + total_sum).astype(jnp.bfloat16))
    return jnp.stack(finished)
```

```python
import functools

import jax
import jax.numpy as jnp
from jax import lax
from jax.experimental import pallas as pl
from jax.experimental.pallas import tpu as pltpu
from jax.sharding import PartitionSpec as P

CAP = 64
CHIPS = 4
RING = 8
EXPERTS = 2 * CHIPS
HOPS = ((0, 0), (1, 0), (3, 0), (1, 1), (3, 1), (0, 1), (2, 0), (2, 1))
NEAR = 6
NEAR_FLOPS, FAR_FLOPS = 2**34, 2**28
AXES = ("section", "expert")
bf16, f32 = jnp.bfloat16, jnp.float32


def params(mib):
    return pltpu.CompilerParams(vmem_limit_bytes=mib * 2**20)


def call(kernel, out_shape, mib, flops=0, nbytes=0):
    return pl.pallas_call(
        kernel,
        out_shape=out_shape,
        compiler_params=params(mib),
        cost_estimate=pl.CostEstimate(flops=flops, bytes_accessed=nbytes, transcendentals=0),
    )


def towards(section, hop, sign):
    x, core = section // 2, section % 2
    return 2 * ((x + sign * hop[0]) % CHIPS) + (core + hop[1]) % 2


def hop_along(array, hop):
    return lax.ppermute(array, "section", [(i, towards(i, hop, 1)) for i in range(EXPERTS)])


def ring_groups():
    def place(section, z, y):
        return section * RING * RING + z * RING + y

    gather, reduce = [], []
    for section in range(EXPERTS):
        for u in range(RING):
            by_z = [place(section, v, u) for v in range(RING)]
            by_y = [place(section, u, v) for v in range(RING)]
            gather.append(by_y if section % 2 else by_z)
            reduce.append(by_z if section % 2 else by_y)
    return gather, reduce


def prep_kernel(tok_ref, gain_ref, router_ref, routing_ref, weight_ref, rank_ref, *packed_refs):
    section = lax.axis_index("section")
    rows = tok_ref.shape[0]
    x = tok_ref[...].astype(f32)
    mean_sq = jnp.mean(x * x, axis=-1, keepdims=True)
    normed = (x * lax.rsqrt(mean_sq + 1e-05) * gain_ref[...].astype(f32)).astype(bf16)

    ids = routing_ref[section]
    labels = lax.broadcasted_iota(jnp.int32, (EXPERTS, rows), 0)
    is_first, is_second = labels == ids[0:1], labels == ids[1:2]
    chosen = jnp.where(is_first | is_second, 1.0, 0.0)
    tall = lax.broadcasted_iota(jnp.int32, (rows, rows), 0)
    wide = lax.broadcasted_iota(jnp.int32, (rows, rows), 1)
    upto = jnp.where(tall <= wide, 1.0, 0.0).astype(bf16)
    ranks = jnp.dot(chosen.astype(bf16), upto, preferred_element_type=f32)
    rank_ref[...] = jnp.where(chosen > 0.0, ranks - 1.0, -1.0)
    slots = lax.broadcasted_iota(jnp.int32, (CAP, rows), 0).astype(f32)
    placing = jnp.concatenate(
        [
            jnp.where(slots == rank_ref[pl.ds(towards(section, hop, 1), 1), :], 1.0, 0.0)
            for hop in HOPS
        ],
        axis=0,
    ).astype(bf16)
    packed = jnp.dot(placing, normed, preferred_element_type=f32).astype(bf16)
    for k, ref in enumerate(packed_refs):
        ref[...] = packed[k * CAP : (k + 1) * CAP]

    logits = lax.dot_general(
        router_ref[...], normed, (((1,), (1,)), ((), ())), preferred_element_type=f32
    )
    margin = jnp.sum(jnp.where(is_first, logits, 0.0), axis=0, keepdims=True) - jnp.sum(
        jnp.where(is_second, logits, 0.0), axis=0, keepdims=True
    )
    weight_ref[...] = jnp.where(
        is_first, jax.nn.sigmoid(margin), jnp.where(is_second, jax.nn.sigmoid(-margin), 0.0)
    )


def regroup_kernel(down_ref, _, out_ref):
    swap = lax.axis_index("section") % 2
    major, minor = jnp.where(swap == 1, RING, 1), jnp.where(swap == 1, 1, RING)
    for p in range(RING):
        for q in range(RING):
            at = pl.multiple_of((p * major + q * minor) * 128, 128)
            out_ref[p, :, q * 128 : (q + 1) * 128] = down_ref[:, pl.ds(at, 128)]


def hidden_rows(gate_ref, up_ref, packed_refs):
    depth, width = gate_ref.shape
    step = 256
    total = None
    for at in range(0, depth, step):
        left = jnp.concatenate([ref[:, at : at + step] for ref in packed_refs], axis=0)
        right = jnp.concatenate([gate_ref[at : at + step], up_ref[at : at + step]], axis=1)
        term = jnp.dot(left, right, preferred_element_type=f32)
        total = term if total is None else total + term
    return (jax.nn.silu(total[:, :width]) * total[:, width:]).astype(bf16)


def near_kernel(gate_ref, up_ref, *rest):
    rest[-1][...] = hidden_rows(gate_ref, up_ref, rest[:-1])


def far_kernel(gate_ref, up_ref, near_ref, *rest):
    split, out_ref = near_ref.shape[0], rest[-1]
    near, far = near_ref[...], hidden_rows(gate_ref, up_ref, rest[:-1])
    for p in range(RING):
        out_ref[p, :split] = near
        out_ref[p, split:] = far


def project_kernel(down_ref, hidden_ref, out_ref):
    blocks, cols, depth = down_ref.shape
    width = hidden_ref.shape[2]
    total = None
    for q in range(0, RING, 2):
        left = down_ref[:, :, q * width : (q + 2) * width].reshape(blocks * cols, 2 * width)
        right = jnp.concatenate([hidden_ref[q], hidden_ref[q + 1]], axis=1)
        term = lax.dot_general(left, right, (((1,), (1,)), ((), ())), preferred_element_type=f32)
        total = term if total is None else total + term
    out_ref[...] = total.astype(bf16).reshape(blocks, cols, -1)


def sum_kernel(parts_ref, out_ref):
    section = lax.axis_index("section")
    total = jnp.sum(parts_ref[...].astype(f32), axis=0).astype(bf16)
    for k, hop in enumerate(HOPS):
        block = total[:, k * CAP : (k + 1) * CAP]
        out_ref[towards(section, hop, -1)] = jnp.concatenate([block, block], axis=1)


def combine_kernel(outputs_ref, weight_ref, rank_ref, own_ref, out_ref):
    rows = own_ref.shape[1]
    slots = lax.broadcasted_iota(jnp.int32, (CAP, rows), 0).astype(f32)
    total = own_ref[...].astype(f32)
    for e in range(EXPERTS):
        placing = jnp.where(slots == rank_ref[e : e + 1, :], 1.0, 0.0).astype(bf16)
        picked = jnp.dot(outputs_ref[e, :, :CAP], placing, preferred_element_type=f32)
        total = total + weight_ref[e : e + 1, :] * picked
    out_ref[...] = total.astype(bf16)


def per_device(tokens, gains, w_router, w_gate, w_up, w_down, routing):
    gather_groups, reduce_groups = ring_groups()
    exchange = functools.partial(
        lax.all_to_all, axis_name=AXES, split_axis=0, concat_axis=0
    )
    rows, depth = tokens.shape[1:]
    width, cols = w_gate.shape[2], w_down.shape[1]
    shape = jax.ShapeDtypeStruct
    block = shape((CAP, depth), bf16)

    weight, rank, *packed = pl.pallas_call(
        prep_kernel,
        out_shape=[shape((EXPERTS, rows), f32)] * 2 + [block] * len(HOPS),
        compiler_params=params(16),
    )(tokens[0], gains[None], w_router.T, jnp.swapaxes(routing, 1, 2))
    arrived = [packed[0]] + [
        hop_along(array, hop) for array, hop in zip(packed[1:], HOPS[1:], strict=True)
    ]

    down = call(regroup_kernel, shape((RING, cols, RING * width), bf16), 8)(w_down[0], rank)
    down = exchange(down, axis_index_groups=reduce_groups)

    slots = len(HOPS) * CAP
    hidden = call(near_kernel, shape((NEAR * CAP, width), bf16), 16, NEAR_FLOPS, 2**22)(
        w_gate[0], w_up[0], *arrived[:NEAR]
    )
    hidden = call(far_kernel, shape((RING, slots, width), bf16), 16, FAR_FLOPS, 2**22)(
        w_gate[0], w_up[0], hidden, *arrived[NEAR:]
    )
    hidden = exchange(hidden, axis_index_groups=gather_groups)
    parts = call(project_kernel, shape((RING, cols, slots), bf16), 16, 2**29, 2**21)(down, hidden)
    parts = exchange(parts, axis_index_groups=reduce_groups)
    outputs = call(sum_kernel, shape((EXPERTS, cols, 2 * CAP), bf16), 8)(parts)
    outputs = lax.all_to_all(outputs, "section", 0, 0)
    own = lax.dynamic_slice_in_dim(tokens[0], lax.axis_index("expert") * cols, cols, 1)
    result = call(combine_kernel, shape((cols, rows), bf16), 8)(outputs, weight, rank, own.T)
    return result.T[None]


def solution(mesh):
    in_specs = (
        P("section", None, None),
        P(),
        P(),
        P("section", None, "expert"),
        P("section", None, "expert"),
        P("section", "expert", None),
        P(),
    )
    out_specs = P("section", None, "expert")
    return jax.shard_map(
        per_device, mesh=mesh, in_specs=in_specs, out_specs=out_specs, check_vma=False
    )
```

```python
import functools

import jax
import jax.numpy as jnp
from jax import lax
from jax.experimental import pallas as pl
from jax.experimental.pallas import tpu as pltpu
from jax.sharding import PartitionSpec as P

CAP = 64
CHIPS = 4
RING = 8
EXPERTS = 2 * CHIPS
HOPS = ((0, 0), (1, 0), (3, 0), (1, 1), (0, 1), (3, 1), (2, 0), (2, 1))
NEAR = 5
NEAR_FLOPS, FAR_FLOPS = 2**34, 2**28
PIECES = 4
FULL = 60
AXES = ("section", "expert")
bf16, f32 = jnp.bfloat16, jnp.float32


def params(mib):
    return pltpu.CompilerParams(vmem_limit_bytes=mib * 2**20)


def call(kernel, out_shape, mib, flops=0, nbytes=0):
    return pl.pallas_call(
        kernel,
        out_shape=out_shape,
        compiler_params=params(mib),
        cost_estimate=pl.CostEstimate(flops=flops, bytes_accessed=nbytes, transcendentals=0),
    )


def towards(section, hop, sign):
    x, core = section // 2, section % 2
    return 2 * ((x + sign * hop[0]) % CHIPS) + (core + hop[1]) % 2


def hop_along(array, hop):
    return lax.ppermute(array, "section", [(i, towards(i, hop, 1)) for i in range(EXPERTS)])


def ring_groups():
    def place(section, z, y):
        return section * RING * RING + z * RING + y

    gather, reduce, wide = [], [], []
    for core in range(2):
        for u in range(RING):
            by_z = [[place(2 * x + core, v, u) for v in range(RING)] for x in range(CHIPS)]
            by_y = [[place(2 * x + core, u, v) for v in range(RING)] for x in range(CHIPS)]
            gather += by_y if core else by_z
            across = by_z if core else by_y
            reduce += across
            wide.append([device for line in across for device in line])
    return gather, reduce, wide


def norm_rows(tok_ref, gain_ref):
    x = tok_ref[...].astype(f32)
    mean_sq = jnp.mean(x * x, axis=-1, keepdims=True)
    return (x * lax.rsqrt(mean_sq + 1e-05) * gain_ref[...].astype(f32)).astype(bf16)


def ranks_of(ids):
    rows = ids.shape[1]
    labels = lax.broadcasted_iota(jnp.int32, (EXPERTS, rows), 0)
    chosen = jnp.where((labels == ids[0:1]) | (labels == ids[1:2]), 1.0, 0.0)
    tall = lax.broadcasted_iota(jnp.int32, (rows, rows), 0)
    wide = lax.broadcasted_iota(jnp.int32, (rows, rows), 1)
    upto = jnp.where(tall <= wide, 1.0, 0.0).astype(bf16)
    ranks = jnp.dot(chosen.astype(bf16), upto, preferred_element_type=f32)
    return jnp.where(chosen > 0.0, ranks - 1.0, -1.0)


def placing_of(rank_row):
    slots = lax.broadcasted_iota(jnp.int32, (CAP, rank_row.shape[1]), 0).astype(f32)
    return jnp.where(slots == rank_row, 1.0, 0.0)


def pack_kernel(tok_ref, gain_ref, routing_ref, *rest):
    packed_refs, rank_ref = rest[:-1], rest[-1]
    section = lax.axis_index("section")
    rank_ref[...] = ranks_of(routing_ref[section])
    placing = jnp.concatenate(
        [placing_of(rank_ref[pl.ds(towards(section, hop, 1), 1), :]) for hop in HOPS[1:]], axis=0
    ).astype(bf16)
    normed = norm_rows(tok_ref, gain_ref)
    packed = jnp.dot(placing, normed, preferred_element_type=f32).astype(bf16)
    for k, ref in enumerate(packed_refs):
        ref[...] = packed[k * CAP : (k + 1) * CAP]


def share_kernel(tok_ref, gain_ref, routing_ref, router_ref, weight_ref, rank_ref, own_ref):
    section = lax.axis_index("section")
    ids = routing_ref[section]
    rank_ref[...] = ranks_of(ids)
    normed = norm_rows(tok_ref, gain_ref)
    placing = placing_of(rank_ref[pl.ds(section, 1), :]).astype(bf16)
    own_ref[...] = jnp.dot(placing, normed, preferred_element_type=f32).astype(bf16)
    logits = lax.dot_general(
        router_ref[...], normed, (((1,), (1,)), ((), ())), preferred_element_type=f32
    )
    labels = lax.broadcasted_iota(jnp.int32, logits.shape, 0)
    is_first, is_second = labels == ids[0:1], labels == ids[1:2]
    margin = jnp.sum(jnp.where(is_first, logits, 0.0), axis=0, keepdims=True) - jnp.sum(
        jnp.where(is_second, logits, 0.0), axis=0, keepdims=True
    )
    weight_ref[...] = jnp.where(
        is_first, jax.nn.sigmoid(margin), jnp.where(is_second, jax.nn.sigmoid(-margin), 0.0)
    )


def regroup_kernel(down_ref, out_ref):
    swap = lax.axis_index("section") % 2
    major, minor = jnp.where(swap == 1, RING, 1), jnp.where(swap == 1, 1, RING)
    for p in range(RING):
        for q in range(RING):
            at = pl.multiple_of((p * major + q * minor) * 128, 128)
            out_ref[p, :, q * 128 : (q + 1) * 128] = down_ref[:, pl.ds(at, 128)]


def hidden_rows(gate, up, block_refs, gate_ref, up_ref, rows_ref, sems):
    depth, width = gate_ref.shape
    piece = depth // PIECES

    def copies(at):
        span = pl.ds(at * piece, piece)
        pairs = [(gate.at[span], gate_ref.at[span]), (up.at[span], up_ref.at[span])] + [
            (ref.at[:, span], rows_ref.at[pl.ds(k * CAP, CAP), span])
            for k, ref in enumerate(block_refs)
        ]
        return [
            pltpu.make_async_copy(source, target, sems.at[at, k])
            for k, (source, target) in enumerate(pairs)
        ]

    landing = [copies(at) for at in range(PIECES)]
    for group in landing:
        for copy in group:
            copy.start()
    total = None
    for at, group in enumerate(landing):
        for copy in group:
            copy.wait()
        for k in range(at * piece, (at + 1) * piece, 256):
            right = jnp.concatenate([gate_ref[k : k + 256], up_ref[k : k + 256]], axis=1)
            term = jnp.dot(rows_ref[:, k : k + 256], right, preferred_element_type=f32)
            total = term if total is None else total + term
    return (jax.nn.silu(total[:, :width]) * total[:, width:]).astype(bf16)


def hidden_kernel(first, gate, up, *rest):
    *block_refs, out_ref, gate_ref, up_ref, rows_ref, made_ref, sems, out_sems = rest
    if first:
        block_refs = block_refs[1:]
    made_ref[...] = hidden_rows(gate, up, block_refs, gate_ref, up_ref, rows_ref, sems)
    copies = [
        pltpu.make_async_copy(
            made_ref, out_ref.at[p, pl.ds(first, made_ref.shape[0])], out_sems.at[p]
        )
        for p in range(RING)
    ]
    for copy in copies:
        copy.start()
    for copy in copies:
        copy.wait()


def project_kernel(down_ref, hidden_ref, out_ref):
    blocks, cols, depth = down_ref.shape
    width = hidden_ref.shape[2]
    total = None
    for q in range(0, RING, 2):
        left = down_ref[:, :, q * width : (q + 2) * width].reshape(blocks * cols, 2 * width)
        right = jnp.concatenate([hidden_ref[q], hidden_ref[q + 1]], axis=1)
        term = lax.dot_general(left, right, (((1,), (1,)), ((), ())), preferred_element_type=f32)
        total = term if total is None else total + term
    parts = total.astype(bf16).reshape(blocks, cols, -1)
    x = lax.axis_index("section") // 2
    for steps in range(CHIPS):
        same, other = HOPS.index((steps, 0)) * CAP, HOPS.index((steps, 1)) * CAP
        pair = [parts[:, :, same : same + CAP], parts[:, :, other : other + CAP]]
        out_ref[pl.ds((x + CHIPS - steps) % CHIPS * RING, RING)] = jnp.concatenate(pair, axis=2)


def sum_kernel(parts_ref, out_ref):
    for x in range(CHIPS):
        total = jnp.sum(parts_ref[x * RING : (x + 1) * RING].astype(f32), axis=0)
        out_ref[x] = total.astype(bf16)


def combine_kernel(mine_ref, theirs_ref, weight_ref, rank_ref, own_ref, out_ref):
    rows = own_ref.shape[1]
    core = lax.axis_index("section") % 2
    slots = lax.broadcasted_iota(jnp.int32, (CAP, rows), 0).astype(f32)
    total = own_ref[...].astype(f32)
    for x in range(CHIPS):
        for ref, at, parity in ((mine_ref, 0, core), (theirs_ref, CAP, 1 - core)):
            row = pl.ds(2 * x + parity, 1)
            placing = jnp.where(slots == rank_ref[row, :], 1.0, 0.0).astype(bf16)
            picked = jnp.dot(ref[x, :, at : at + CAP], placing, preferred_element_type=f32)
            total = total + weight_ref[row, :] * picked
    out_ref[...] = total.astype(bf16)


def hidden_of(gate, up, slots, flops, first, before, blocks):
    depth, width = gate.shape
    operands = [gate, up, *before, *blocks]
    return pl.pallas_call(
        functools.partial(hidden_kernel, first),
        out_shape=jax.ShapeDtypeStruct((RING, slots, width), bf16),
        in_specs=[pl.BlockSpec(memory_space=pl.ANY)] * len(operands),
        out_specs=pl.BlockSpec(memory_space=pl.ANY),
        scratch_shapes=[
            pltpu.VMEM(gate.shape, bf16),
            pltpu.VMEM(gate.shape, bf16),
            pltpu.VMEM((len(blocks) * CAP, depth), bf16),
            pltpu.VMEM((len(blocks) * CAP, width), bf16),
            pltpu.SemaphoreType.DMA((PIECES, 2 + len(blocks))),
            pltpu.SemaphoreType.DMA((RING,)),
        ],
        input_output_aliases={2: 0} if before else {},
        compiler_params=params(FULL),
        cost_estimate=pl.CostEstimate(flops=flops, bytes_accessed=2**22, transcendentals=0),
    )(*operands)


def per_device(tokens, gains, w_router, w_gate, w_up, w_down, routing):
    gather_groups, reduce_groups, wide_groups = ring_groups()
    exchange = functools.partial(
        lax.all_to_all, axis_name=AXES, split_axis=0, concat_axis=0
    )
    rows, depth = tokens.shape[1:]
    width, cols = w_gate.shape[2], w_down.shape[1]
    shape = jax.ShapeDtypeStruct
    block = shape((CAP, depth), bf16)

    ids = jnp.swapaxes(routing, 1, 2)
    packed = pl.pallas_call(
        pack_kernel,
        out_shape=[block] * (len(HOPS) - 1),
        scratch_shapes=[pltpu.VMEM((EXPERTS, rows), f32)],
        compiler_params=params(12),
    )(tokens[0], gains, ids)
    arrived = [hop_along(array, hop) for array, hop in zip(packed, HOPS[1:], strict=True)]
    late_tokens, _ = lax.optimization_barrier((tokens[0], arrived[0]))
    late_down, *_ = lax.optimization_barrier((w_down[0], *arrived[:3]))
    weight, rank, own = pl.pallas_call(
        share_kernel,
        out_shape=[shape((EXPERTS, rows), f32)] * 2 + [block],
        compiler_params=params(12),
    )(late_tokens, gains, ids, w_router.T)
    down = call(regroup_kernel, shape((RING, cols, RING * width), bf16), 8)(late_down)
    down = exchange(down, axis_index_groups=reduce_groups)

    slots = len(HOPS) * CAP
    near, far = [own] + arrived[: NEAR - 1], arrived[NEAR - 1 :]
    hidden_call = functools.partial(hidden_of, w_gate[0], w_up[0], slots)
    hidden = hidden_call(NEAR_FLOPS, 0, [], near)
    hidden = hidden_call(FAR_FLOPS, NEAR * CAP, [hidden], far)
    hidden = exchange(hidden, axis_index_groups=gather_groups)
    pair = (CHIPS * RING, cols, 2 * CAP)
    parts = call(project_kernel, shape(pair, bf16), 16, 2**29, 2**21)(down, hidden)
    parts = exchange(parts, axis_index_groups=wide_groups)
    mine = call(sum_kernel, shape((CHIPS, cols, 2 * CAP), bf16), 8)(parts)
    theirs = hop_along(mine, (0, 1))
    own = lax.dynamic_slice_in_dim(tokens[0], lax.axis_index("expert") * cols, cols, 1)
    result = call(combine_kernel, shape((cols, rows), bf16), 8)(mine, theirs, weight, rank, own.T)
    return result.T[None]


def solution(mesh):
    in_specs = (
        P("section", None, None),
        P(),
        P(),
        P("section", None, "expert"),
        P("section", None, "expert"),
        P("section", "expert", None),
        P(),
    )
    out_specs = P("section", None, "expert")
    return jax.shard_map(
        per_device, mesh=mesh, in_specs=in_specs, out_specs=out_specs, check_vma=False
    )
```

```python
import functools

import jax
import jax.numpy as jnp
from jax import lax
from jax.experimental import pallas as pl
from jax.experimental.pallas import tpu as pltpu
from jax.sharding import PartitionSpec as P

CAP = 64
CHIPS = 4
RING = 8
EXPERTS = 2 * CHIPS
HOPS = ((0, 0), (1, 0), (3, 0), (1, 1), (0, 1), (3, 1), (2, 0), (2, 1))
NEAR = 5
NEAR_FLOPS, FAR_FLOPS = 2**34, 2**28
PIECES = 2
FULL = 60
AXES = ("section", "expert")
bf16, f32 = jnp.bfloat16, jnp.float32


def params(mib):
    return pltpu.CompilerParams(vmem_limit_bytes=mib * 2**20)


def call(kernel, out_shape, mib, flops=0, nbytes=0):
    return pl.pallas_call(
        kernel,
        out_shape=out_shape,
        compiler_params=params(mib),
        cost_estimate=pl.CostEstimate(flops=flops, bytes_accessed=nbytes, transcendentals=0),
    )


def towards(section, hop, sign):
    x, core = section // 2, section % 2
    return 2 * ((x + sign * hop[0]) % CHIPS) + (core + hop[1]) % 2


def hop_along(array, hop):
    return lax.ppermute(array, "section", [(i, towards(i, hop, 1)) for i in range(EXPERTS)])


def ring_groups():
    def place(section, z, y):
        return section * RING * RING + z * RING + y

    gather, reduce, wide = [], [], []
    for core in range(2):
        for u in range(RING):
            by_z = [[place(2 * x + core, v, u) for v in range(RING)] for x in range(CHIPS)]
            by_y = [[place(2 * x + core, u, v) for v in range(RING)] for x in range(CHIPS)]
            gather += by_y if core else by_z
            across = by_z if core else by_y
            reduce += across
            wide.append([device for line in across for device in line])
    return gather, reduce, wide


def norm_rows(tok_ref, gain_ref):
    x = tok_ref[...].astype(f32)
    mean_sq = jnp.mean(x * x, axis=-1, keepdims=True)
    return (x * lax.rsqrt(mean_sq + 1e-05) * gain_ref[...].astype(f32)).astype(bf16)


def ranks_of(ids):
    rows = ids.shape[1]
    labels = lax.broadcasted_iota(jnp.int32, (EXPERTS, rows), 0)
    chosen = jnp.where((labels == ids[0:1]) | (labels == ids[1:2]), 1.0, 0.0)
    tall = lax.broadcasted_iota(jnp.int32, (rows, rows), 0)
    wide = lax.broadcasted_iota(jnp.int32, (rows, rows), 1)
    upto = jnp.where(tall <= wide, 1.0, 0.0).astype(bf16)
    ranks = jnp.dot(chosen.astype(bf16), upto, preferred_element_type=f32)
    return jnp.where(chosen > 0.0, ranks - 1.0, -1.0)


def placing_of(rank_row):
    slots = lax.broadcasted_iota(jnp.int32, (CAP, rank_row.shape[1]), 0).astype(f32)
    return jnp.where(slots == rank_row, 1.0, 0.0)


def pack_kernel(tok_ref, gain_ref, routing_ref, *rest):
    packed_refs, rank_ref = rest[:-1], rest[-1]
    section = lax.axis_index("section")
    rank_ref[...] = ranks_of(routing_ref[section])
    placing = jnp.concatenate(
        [placing_of(rank_ref[pl.ds(towards(section, hop, 1), 1), :]) for hop in HOPS[1:]], axis=0
    ).astype(bf16)
    normed = norm_rows(tok_ref, gain_ref)
    packed = jnp.dot(placing, normed, preferred_element_type=f32).astype(bf16)
    for k, ref in enumerate(packed_refs):
        ref[...] = packed[k * CAP : (k + 1) * CAP]


def share_kernel(tok_ref, gain_ref, routing_ref, router_ref, weight_ref, rank_ref, own_ref):
    section = lax.axis_index("section")
    ids = routing_ref[section]
    rank_ref[...] = ranks_of(ids)
    normed = norm_rows(tok_ref, gain_ref)
    placing = placing_of(rank_ref[pl.ds(section, 1), :]).astype(bf16)
    own_ref[...] = jnp.dot(placing, normed, preferred_element_type=f32).astype(bf16)
    logits = lax.dot_general(
        router_ref[...], normed, (((1,), (1,)), ((), ())), preferred_element_type=f32
    )
    labels = lax.broadcasted_iota(jnp.int32, logits.shape, 0)
    is_first, is_second = labels == ids[0:1], labels == ids[1:2]
    margin = jnp.sum(jnp.where(is_first, logits, 0.0), axis=0, keepdims=True) - jnp.sum(
        jnp.where(is_second, logits, 0.0), axis=0, keepdims=True
    )
    weight_ref[...] = jnp.where(
        is_first, jax.nn.sigmoid(margin), jnp.where(is_second, jax.nn.sigmoid(-margin), 0.0)
    )


def regroup_kernel(down_ref, out_ref):
    swap = lax.axis_index("section") % 2
    major, minor = jnp.where(swap == 1, RING, 1), jnp.where(swap == 1, 1, RING)
    for p in range(RING):
        for q in range(RING):
            at = pl.multiple_of((p * major + q * minor) * 128, 128)
            out_ref[p, :, q * 128 : (q + 1) * 128] = down_ref[:, pl.ds(at, 128)]


def hidden_rows(gate, up, block_refs, gate_ref, up_ref, rows_ref, sems):
    depth, width = gate_ref.shape
    piece = depth // PIECES

    def copies(at):
        span = pl.ds(at * piece, piece)
        pairs = [(gate.at[span], gate_ref.at[span]), (up.at[span], up_ref.at[span])] + [
            (ref.at[:, span], rows_ref.at[pl.ds(k * CAP, CAP), span])
            for k, ref in enumerate(block_refs)
        ]
        return [
            pltpu.make_async_copy(source, target, sems.at[at, k])
            for k, (source, target) in enumerate(pairs)
        ]

    landing = [copies(at) for at in range(PIECES)]
    for group in landing:
        for copy in group:
            copy.start()
    total = None
    for at, group in enumerate(landing):
        for copy in group:
            copy.wait()
        for k in range(at * piece, (at + 1) * piece, 256):
            right = jnp.concatenate([gate_ref[k : k + 256], up_ref[k : k + 256]], axis=1)
            term = jnp.dot(rows_ref[:, k : k + 256], right, preferred_element_type=f32)
            total = term if total is None else total + term
    return (jax.nn.silu(total[:, :width]) * total[:, width:]).astype(bf16)


def hidden_kernel(first, gate, up, *rest):
    *block_refs, out_ref, gate_ref, up_ref, rows_ref, made_ref, sems, out_sems = rest
    if first:
        block_refs = block_refs[1:]
    made_ref[...] = hidden_rows(gate, up, block_refs, gate_ref, up_ref, rows_ref, sems)
    copies = [
        pltpu.make_async_copy(
            made_ref, out_ref.at[p, pl.ds(first, made_ref.shape[0])], out_sems.at[p]
        )
        for p in range(RING)
    ]
    for copy in copies:
        copy.start()
    for copy in copies:
        copy.wait()


def project_kernel(down_ref, hidden_ref, out_ref):
    blocks, cols, depth = down_ref.shape
    width = hidden_ref.shape[2]
    total = None
    for q in range(0, RING, 2):
        left = down_ref[:, :, q * width : (q + 2) * width].reshape(blocks * cols, 2 * width)
        right = jnp.concatenate([hidden_ref[q], hidden_ref[q + 1]], axis=1)
        term = lax.dot_general(left, right, (((1,), (1,)), ((), ())), preferred_element_type=f32)
        total = term if total is None else total + term
    parts = total.astype(bf16).reshape(blocks, cols, -1)
    x = lax.axis_index("section") // 2
    for steps in range(CHIPS):
        same, other = HOPS.index((steps, 0)) * CAP, HOPS.index((steps, 1)) * CAP
        pair = [parts[:, :, same : same + CAP], parts[:, :, other : other + CAP]]
        out_ref[pl.ds((x + CHIPS - steps) % CHIPS * RING, RING)] = jnp.concatenate(pair, axis=2)


def sum_kernel(parts_ref, out_ref):
    for x in range(CHIPS):
        total = jnp.sum(parts_ref[x * RING : (x + 1) * RING].astype(f32), axis=0)
        out_ref[x] = total.astype(bf16)


def combine_kernel(mine_ref, theirs_ref, weight_ref, rank_ref, own_ref, out_ref):
    rows = own_ref.shape[1]
    core = lax.axis_index("section") % 2
    slots = lax.broadcasted_iota(jnp.int32, (CAP, rows), 0).astype(f32)
    total = own_ref[...].astype(f32)
    for x in range(CHIPS):
        for ref, at, parity in ((mine_ref, 0, core), (theirs_ref, CAP, 1 - core)):
            row = pl.ds(2 * x + parity, 1)
            placing = jnp.where(slots == rank_ref[row, :], 1.0, 0.0).astype(bf16)
            picked = jnp.dot(ref[x, :, at : at + CAP], placing, preferred_element_type=f32)
            total = total + weight_ref[row, :] * picked
    out_ref[...] = total.astype(bf16)


def hidden_of(gate, up, slots, flops, first, before, blocks):
    depth, width = gate.shape
    operands = [gate, up, *before, *blocks]
    return pl.pallas_call(
        functools.partial(hidden_kernel, first),
        out_shape=jax.ShapeDtypeStruct((RING, slots, width), bf16),
        in_specs=[pl.BlockSpec(memory_space=pl.ANY)] * len(operands),
        out_specs=pl.BlockSpec(memory_space=pl.ANY),
        scratch_shapes=[
            pltpu.VMEM(gate.shape, bf16),
            pltpu.VMEM(gate.shape, bf16),
            pltpu.VMEM((len(blocks) * CAP, depth), bf16),
            pltpu.VMEM((len(blocks) * CAP, width), bf16),
            pltpu.SemaphoreType.DMA((PIECES, 2 + len(blocks))),
            pltpu.SemaphoreType.DMA((RING,)),
        ],
        input_output_aliases={2: 0} if before else {},
        compiler_params=params(FULL),
        cost_estimate=pl.CostEstimate(flops=flops, bytes_accessed=2**22, transcendentals=0),
    )(*operands)


def per_device(tokens, gains, w_router, w_gate, w_up, w_down, routing):
    gather_groups, reduce_groups, wide_groups = ring_groups()
    exchange = functools.partial(
        lax.all_to_all, axis_name=AXES, split_axis=0, concat_axis=0
    )
    rows, depth = tokens.shape[1:]
    width, cols = w_gate.shape[2], w_down.shape[1]
    shape = jax.ShapeDtypeStruct
    block = shape((CAP, depth), bf16)

    ids = jnp.swapaxes(routing, 1, 2)
    packed = pl.pallas_call(
        pack_kernel,
        out_shape=[block] * (len(HOPS) - 1),
        scratch_shapes=[pltpu.VMEM((EXPERTS, rows), f32)],
        compiler_params=params(12),
    )(tokens[0], gains, ids)
    arrived = [hop_along(array, hop) for array, hop in zip(packed, HOPS[1:], strict=True)]
    late_tokens, _ = lax.optimization_barrier((tokens[0], arrived[0]))
    late_down, *_ = lax.optimization_barrier((w_down[0], *arrived[:3]))
    weight, rank, own = pl.pallas_call(
        share_kernel,
        out_shape=[shape((EXPERTS, rows), f32)] * 2 + [block],
        compiler_params=params(12),
    )(late_tokens, gains, ids, w_router.T)
    down = call(regroup_kernel, shape((RING, cols, RING * width), bf16), 8)(late_down)
    down = exchange(down, axis_index_groups=reduce_groups)

    slots = len(HOPS) * CAP
    near, far = [own] + arrived[: NEAR - 1], arrived[NEAR - 1 :]
    hidden_call = functools.partial(hidden_of, w_gate[0], w_up[0], slots)
    hidden = hidden_call(NEAR_FLOPS, 0, [], near)
    hidden = hidden_call(FAR_FLOPS, NEAR * CAP, [hidden], far)
    hidden = exchange(hidden, axis_index_groups=gather_groups)
    pair = (CHIPS * RING, cols, 2 * CAP)
    parts = call(project_kernel, shape(pair, bf16), 16, 2**29, 2**21)(down, hidden)
    parts = exchange(parts, axis_index_groups=wide_groups)
    mine = call(sum_kernel, shape((CHIPS, cols, 2 * CAP), bf16), 8)(parts)
    theirs = hop_along(mine, (0, 1))
    own = lax.dynamic_slice_in_dim(tokens[0], lax.axis_index("expert") * cols, cols, 1)
    result = call(combine_kernel, shape((cols, rows), bf16), 8)(mine, theirs, weight, rank, own.T)
    return result.T[None]


def solution(mesh):
    in_specs = (
        P("section", None, None),
        P(),
        P(),
        P("section", None, "expert"),
        P("section", None, "expert"),
        P("section", "expert", None),
        P(),
    )
    out_specs = P("section", None, "expert")
    return jax.shard_map(
        per_device, mesh=mesh, in_specs=in_specs, out_specs=out_specs, check_vma=False
    )
```

```python
import functools

import jax
import jax.numpy as jnp
from jax import lax
from jax.experimental import pallas as pl
from jax.experimental.pallas import tpu as pltpu
from jax.sharding import PartitionSpec as P

CAP = 64
CHIPS = 4
RING = 8
EXPERTS = 2 * CHIPS
HOPS = ((0, 0), (1, 0), (3, 0), (1, 1), (0, 1), (3, 1), (2, 0), (2, 1))
NEAR = 5
NEAR_FLOPS, FAR_FLOPS = 2**34, 2**28
PIECES = 4
FULL = 60
AXES = ("section", "expert")
bf16, f32 = jnp.bfloat16, jnp.float32


def params(mib):
    return pltpu.CompilerParams(vmem_limit_bytes=mib * 2**20)


def call(kernel, out_shape, mib, flops=0, nbytes=0):
    return pl.pallas_call(
        kernel,
        out_shape=out_shape,
        compiler_params=params(mib),
        cost_estimate=pl.CostEstimate(flops=flops, bytes_accessed=nbytes, transcendentals=0),
    )


def towards(section, hop, sign):
    x, core = section // 2, section % 2
    return 2 * ((x + sign * hop[0]) % CHIPS) + (core + hop[1]) % 2


def hop_along(array, hop):
    return lax.ppermute(array, "section", [(i, towards(i, hop, 1)) for i in range(EXPERTS)])


def ring_groups():
    def place(section, z, y):
        return section * RING * RING + z * RING + y

    gather, reduce, wide = [], [], []
    for core in range(2):
        for u in range(RING):
            by_z = [[place(2 * x + core, v, u) for v in range(RING)] for x in range(CHIPS)]
            by_y = [[place(2 * x + core, u, v) for v in range(RING)] for x in range(CHIPS)]
            gather += by_y if core else by_z
            across = by_z if core else by_y
            reduce += across
            wide.append([device for line in across for device in line])
    return gather, reduce, wide


def norm_rows(tok_ref, gain_ref):
    x = tok_ref[...].astype(f32)
    mean_sq = jnp.mean(x * x, axis=-1, keepdims=True)
    return (x * lax.rsqrt(mean_sq + 1e-05) * gain_ref[...].astype(f32)).astype(bf16)


def ranks_of(ids):
    rows = ids.shape[1]
    labels = lax.broadcasted_iota(jnp.int32, (EXPERTS, rows), 0)
    chosen = jnp.where((labels == ids[0:1]) | (labels == ids[1:2]), 1.0, 0.0)
    tall = lax.broadcasted_iota(jnp.int32, (rows, rows), 0)
    wide = lax.broadcasted_iota(jnp.int32, (rows, rows), 1)
    upto = jnp.where(tall <= wide, 1.0, 0.0).astype(bf16)
    ranks = jnp.dot(chosen.astype(bf16), upto, preferred_element_type=f32)
    return jnp.where(chosen > 0.0, ranks - 1.0, -1.0)


def placing_of(rank_row):
    slots = lax.broadcasted_iota(jnp.int32, (CAP, rank_row.shape[1]), 0).astype(f32)
    return jnp.where(slots == rank_row, 1.0, 0.0)


def pack_kernel(tok_ref, gain_ref, routing_ref, *rest):
    packed_refs, rank_ref = rest[:-1], rest[-1]
    section = lax.axis_index("section")
    rank_ref[...] = ranks_of(routing_ref[section])
    placing = jnp.concatenate(
        [placing_of(rank_ref[pl.ds(towards(section, hop, 1), 1), :]) for hop in HOPS[1:]], axis=0
    ).astype(bf16)
    normed = norm_rows(tok_ref, gain_ref)
    packed = jnp.dot(placing, normed, preferred_element_type=f32).astype(bf16)
    for k, ref in enumerate(packed_refs):
        ref[...] = packed[k * CAP : (k + 1) * CAP]


def share_kernel(tok_ref, gain_ref, routing_ref, router_ref, weight_ref, rank_ref, own_ref):
    section = lax.axis_index("section")
    ids = routing_ref[section]
    rank_ref[...] = ranks_of(ids)
    normed = norm_rows(tok_ref, gain_ref)
    placing = placing_of(rank_ref[pl.ds(section, 1), :]).astype(bf16)
    own_ref[...] = jnp.dot(placing, normed, preferred_element_type=f32).astype(bf16)
    logits = lax.dot_general(
        router_ref[...], normed, (((1,), (1,)), ((), ())), preferred_element_type=f32
    )
    labels = lax.broadcasted_iota(jnp.int32, logits.shape, 0)
    is_first, is_second = labels == ids[0:1], labels == ids[1:2]
    margin = jnp.sum(jnp.where(is_first, logits, 0.0), axis=0, keepdims=True) - jnp.sum(
        jnp.where(is_second, logits, 0.0), axis=0, keepdims=True
    )
    weight_ref[...] = jnp.where(
        is_first, jax.nn.sigmoid(margin), jnp.where(is_second, jax.nn.sigmoid(-margin), 0.0)
    )


def regroup_kernel(down_ref, out_ref):
    swap = lax.axis_index("section") % 2
    major, minor = jnp.where(swap == 1, RING, 1), jnp.where(swap == 1, 1, RING)
    for p in range(RING):
        for q in range(RING):
            at = pl.multiple_of((p * major + q * minor) * 128, 128)
            out_ref[p, :, q * 128 : (q + 1) * 128] = down_ref[:, pl.ds(at, 128)]


def hidden_rows(gate, up, block_refs, gate_ref, up_ref, rows_ref, sems):
    depth, width = gate_ref.shape
    piece = depth // PIECES

    def copies(at):
        span = pl.ds(at * piece, piece)
        pairs = [(gate.at[span], gate_ref.at[span]), (up.at[span], up_ref.at[span])] + [
            (ref.at[:, span], rows_ref.at[pl.ds(k * CAP, CAP), span])
            for k, ref in enumerate(block_refs)
        ]
        return [
            pltpu.make_async_copy(source, target, sems.at[at, k])
            for k, (source, target) in enumerate(pairs)
        ]

    landing = [copies(at) for at in range(PIECES)]
    for group in landing:
        for copy in group:
            copy.start()
    total = None
    for at, group in enumerate(landing):
        for copy in group:
            copy.wait()
        span = pl.ds(at * piece, piece)
        right = jnp.concatenate([gate_ref[span], up_ref[span]], axis=1)
        term = jnp.dot(rows_ref[:, span], right, preferred_element_type=f32)
        total = term if total is None else total + term
    return (jax.nn.silu(total[:, :width]) * total[:, width:]).astype(bf16)


def hidden_kernel(first, gate, up, *rest):
    *block_refs, out_ref, gate_ref, up_ref, rows_ref, made_ref, sems, out_sems = rest
    if first:
        block_refs = block_refs[1:]
    made_ref[...] = hidden_rows(gate, up, block_refs, gate_ref, up_ref, rows_ref, sems)
    copies = [
        pltpu.make_async_copy(
            made_ref, out_ref.at[p, pl.ds(first, made_ref.shape[0])], out_sems.at[p]
        )
        for p in range(RING)
    ]
    for copy in copies:
        copy.start()
    for copy in copies:
        copy.wait()


def project_kernel(down_ref, hidden_ref, out_ref):
    blocks, cols, depth = down_ref.shape
    left = down_ref[...].reshape(blocks * cols, depth)
    right = jnp.concatenate([hidden_ref[q] for q in range(RING)], axis=1)
    total = lax.dot_general(left, right, (((1,), (1,)), ((), ())), preferred_element_type=f32)
    parts = total.astype(bf16).reshape(blocks, cols, -1)
    x = lax.axis_index("section") // 2
    for steps in range(CHIPS):
        same, other = HOPS.index((steps, 0)) * CAP, HOPS.index((steps, 1)) * CAP
        pair = [parts[:, :, same : same + CAP], parts[:, :, other : other + CAP]]
        out_ref[pl.ds((x + CHIPS - steps) % CHIPS * RING, RING)] = jnp.concatenate(pair, axis=2)


def sum_kernel(parts_ref, out_ref):
    for x in range(CHIPS):
        total = jnp.sum(parts_ref[x * RING : (x + 1) * RING].astype(f32), axis=0)
        out_ref[x] = total.astype(bf16)


def combine_kernel(mine_ref, theirs_ref, weight_ref, rank_ref, own_ref, out_ref):
    rows = own_ref.shape[1]
    core = lax.axis_index("section") % 2
    slots = lax.broadcasted_iota(jnp.int32, (CAP, rows), 0).astype(f32)
    total = own_ref[...].astype(f32)
    for x in range(CHIPS):
        for ref, at, parity in ((mine_ref, 0, core), (theirs_ref, CAP, 1 - core)):
            row = pl.ds(2 * x + parity, 1)
            placing = jnp.where(slots == rank_ref[row, :], 1.0, 0.0).astype(bf16)
            picked = jnp.dot(ref[x, :, at : at + CAP], placing, preferred_element_type=f32)
            total = total + weight_ref[row, :] * picked
    out_ref[...] = total.astype(bf16)


def hidden_of(gate, up, slots, flops, first, before, blocks):
    depth, width = gate.shape
    operands = [gate, up, *before, *blocks]
    return pl.pallas_call(
        functools.partial(hidden_kernel, first),
        out_shape=jax.ShapeDtypeStruct((RING, slots, width), bf16),
        in_specs=[pl.BlockSpec(memory_space=pl.ANY)] * len(operands),
        out_specs=pl.BlockSpec(memory_space=pl.ANY),
        scratch_shapes=[
            pltpu.VMEM(gate.shape, bf16),
            pltpu.VMEM(gate.shape, bf16),
            pltpu.VMEM((len(blocks) * CAP, depth), bf16),
            pltpu.VMEM((len(blocks) * CAP, width), bf16),
            pltpu.SemaphoreType.DMA((PIECES, 2 + len(blocks))),
            pltpu.SemaphoreType.DMA((RING,)),
        ],
        input_output_aliases={2: 0} if before else {},
        compiler_params=params(FULL),
        cost_estimate=pl.CostEstimate(flops=flops, bytes_accessed=2**22, transcendentals=0),
    )(*operands)


def per_device(tokens, gains, w_router, w_gate, w_up, w_down, routing):
    gather_groups, reduce_groups, wide_groups = ring_groups()
    exchange = functools.partial(
        lax.all_to_all, axis_name=AXES, split_axis=0, concat_axis=0
    )
    rows, depth = tokens.shape[1:]
    width, cols = w_gate.shape[2], w_down.shape[1]
    shape = jax.ShapeDtypeStruct
    block = shape((CAP, depth), bf16)

    ids = jnp.swapaxes(routing, 1, 2)
    packed = pl.pallas_call(
        pack_kernel,
        out_shape=[block] * (len(HOPS) - 1),
        scratch_shapes=[pltpu.VMEM((EXPERTS, rows), f32)],
        compiler_params=params(12),
    )(tokens[0], gains, ids)
    arrived = [hop_along(array, hop) for array, hop in zip(packed, HOPS[1:], strict=True)]
    late_tokens, _ = lax.optimization_barrier((tokens[0], arrived[0]))
    late_down, *_ = lax.optimization_barrier((w_down[0], *arrived[:3]))
    weight, rank, own = pl.pallas_call(
        share_kernel,
        out_shape=[shape((EXPERTS, rows), f32)] * 2 + [block],
        compiler_params=params(12),
    )(late_tokens, gains, ids, w_router.T)
    down = call(regroup_kernel, shape((RING, cols, RING * width), bf16), 8)(late_down)
    down = exchange(down, axis_index_groups=reduce_groups)

    slots = len(HOPS) * CAP
    near, far = [own] + arrived[: NEAR - 1], arrived[NEAR - 1 :]
    hidden_call = functools.partial(hidden_of, w_gate[0], w_up[0], slots)
    hidden = hidden_call(NEAR_FLOPS, 0, [], near)
    hidden = hidden_call(FAR_FLOPS, NEAR * CAP, [hidden], far)
    hidden = exchange(hidden, axis_index_groups=gather_groups)
    pair = (CHIPS * RING, cols, 2 * CAP)
    parts = call(project_kernel, shape(pair, bf16), 16, 2**29, 2**21)(down, hidden)
    parts = exchange(parts, axis_index_groups=wide_groups)
    mine = call(sum_kernel, shape((CHIPS, cols, 2 * CAP), bf16), 8)(parts)
    theirs = hop_along(mine, (0, 1))
    own = lax.dynamic_slice_in_dim(tokens[0], lax.axis_index("expert") * cols, cols, 1)
    result = call(combine_kernel, shape((cols, rows), bf16), 8)(mine, theirs, weight, rank, own.T)
    return result.T[None]


def solution(mesh):
    in_specs = (
        P("section", None, None),
        P(),
        P(),
        P("section", None, "expert"),
        P("section", None, "expert"),
        P("section", "expert", None),
        P(),
    )
    out_specs = P("section", None, "expert")
    return jax.shard_map(
        per_device, mesh=mesh, in_specs=in_specs, out_specs=out_specs, check_vma=False
    )
```
